32 devices in a mesh: area: 8 (over z, x), unit: 4 (over y, core).
Axes of the slice: x: 2, y: 2, z: 4, core: 2. Of those that a mesh axis runs over, the one named last changes fastest.
Arguments:
- initial_rates: float32 [8, 4096, 128], P('area', 'unit'), may hold values from -0.9 to 0.9
- prior_rates: bfloat16 [8, 4096, 128], P('area', 'unit'), may hold values from -0.8984375 to 0.8984375
- local_weight: bfloat16 [8, 4096, 4096], P('area', 'unit'), may hold values from -0.125 to 0.125
- long_weight: bfloat16 [8, 4096, 2048], P('area', 'unit'), may hold values from -0.1875 to 0.1875
- input_weight: bfloat16 [8, 4096, 16], P('area', 'unit'), may hold values from -1.5 to 1.5
- unit_bias: float32 [8, 4096], P('area', 'unit'), may hold values from -2.5 to 2.5
- leak_rate: float32 [8, 4096], P('area', 'unit'), may hold values from 0.2 to 1
- stimulus: bfloat16 [6, 16, 128], replicated, may hold values from -4 to 4
- link_source: int32 [8, 16], replicated, may hold values from 0 to 7, as said below
- link_block: int32 [8, 16], replicated, may hold values from 0 to 31
- link_delay: int32 [8, 16], replicated, may hold values from 0 to 1
Outputs:
- final_rates: float32 [8, 4096, 128], P('area', 'unit')
- final_current: float32 [8, 4096, 128], P('area', 'unit')
The draws below stay inside these ranges and needn't reach their ends.
Inputs may be any that keep to these rules, and one draw needn't show every extreme that they name: `link_source`: each area's 16 entries name every source area at most 2 times, and some source area exactly 2 times.
All inputs are finite; a program needn't handle non-finite values.
Results may differ from the reference program's by a relative error of at most 0.004.
Values may be sent and summed in bfloat16 or wider, within the bound.
A program may use at most 64 MiB of HBM per device.

```python
import math
import jax
import jax.numpy as jnp
from jax import lax

UNITS = 4096
BLOCK = 128
SLOTS = 16
STIM = 16
WINDOWS = 3
TRIALS = 128
AREAS = 8
INPUTS = 2048
STEPS = 6


def draw_link_source(key, part):
    per_pair = max(1, (SLOTS + AREAS - 1) // AREAS)
    candidates = AREAS * per_pair
    first_key, second_key = jax.random.split(jax.random.fold_in(key, 11))
    favour = jax.random.randint(first_key, (AREAS,), 0, 4) * 400
    jitter = jax.random.randint(second_key, (AREAS, candidates), 0, 1000)
    area_of = jnp.arange(candidates, dtype=jnp.int32) // per_pair
    scores = (jitter + favour[area_of][None, :]) * candidates + jnp.arange(candidates, dtype=jnp.int32)[None, :]
    ignored, picked = lax.top_k(scores, SLOTS)
    return (picked // per_pair).astype(jnp.int32)


def with_ends(array, own_key, smallest, top_value):
    longest = array.shape.index(max(array.shape))
    spots = []
    for shift in (0, 1):
        where = [jax.random.randint(jax.random.fold_in(own_key, axis), (), 0, length) for axis, length in enumerate(array.shape)]
        where[longest] = (where[longest] + shift) % array.shape[longest]
        spots.append(tuple(where))
    return array.at[spots[0]].set(smallest).at[spots[1]].set(top_value)


def steps_of(own_key, shape, cuts, smallest, largest):
    gain = 1.0
    for axis_at, parts in cuts:
        steps = jax.random.uniform(jax.random.fold_in(jax.random.fold_in(own_key, 6), axis_at), (parts,), jnp.float32, smallest / len(cuts), largest / len(cuts))
        gain = gain * jnp.repeat(jnp.exp(steps), shape[axis_at] // parts).reshape((-1,) + (1,) * (len(shape) - 1 - axis_at))
    return gain


def scatter_about(rng, extent, scale, most, cuts=(), kind=jnp.bfloat16):
    level = steps_of(rng, extent, cuts, -0.22, 0.18) if cuts else 1.0
    drawn = jax.random.normal(rng, extent, jnp.float32) * scale * level
    return jnp.minimum(jnp.maximum(drawn, -most), most).astype(kind)


def setup_inputs(seed: int = 0) -> dict:
    key_of = jax.random.split(jax.random.key(seed), 12)
    initial_rates = jnp.clip(jax.random.uniform(key_of[0], (AREAS, UNITS, TRIALS), jnp.float32, -0.9, 0.9) * steps_of(key_of[0], (AREAS, UNITS, TRIALS), ((0, 8), (1, 4)), -0.4, 0.0), -0.9, 0.9)
    prior_rates = jnp.clip(jax.random.uniform(key_of[1], (AREAS, UNITS, TRIALS), jnp.float32, -0.8984375, 0.8984375) * steps_of(key_of[1], (AREAS, UNITS, TRIALS), ((0, 8), (1, 4)), -0.4, 0.0), -0.8984375, 0.8984375).astype(jnp.bfloat16)
    local_weight = scatter_about(key_of[2], (AREAS, UNITS, UNITS), (UNITS // 2) ** -0.5, 0.125, ((0, 8), (1, 4)))
    long_weight = scatter_about(key_of[3], (AREAS, UNITS, INPUTS), (INPUTS // 2) ** -0.5, 0.1875, ((0, 8), (1, 4)))
    input_weight = scatter_about(key_of[4], (AREAS, UNITS, STIM), STIM ** -0.5, 1.5, ((0, 8), (1, 4)))
    unit_bias = scatter_about(key_of[5], (AREAS, UNITS), 0.3, 2.5, ((0, 8), (1, 4)), jnp.float32)
    leak_rate = jnp.clip(jnp.exp(math.log(1.0) - 1.609438 * jax.random.uniform(key_of[6], (AREAS, UNITS), jnp.float32) ** steps_of(key_of[6], (AREAS, UNITS), ((0, 8), (1, 4)), -0.2, 0.2)), 0.2, 1.0)
    stimulus = scatter_about(key_of[7], (STEPS, STIM, TRIALS), 1.0, 4.0)
    link_source = draw_link_source(jax.random.fold_in(key_of[11], 71), 0)
    link_block = with_ends(jax.random.randint(key_of[9], (AREAS, SLOTS), 0, UNITS // BLOCK), jax.random.fold_in(key_of[9], 1), 0, (UNITS // BLOCK) - 1).astype(jnp.int32)
    link_delay = with_ends(jax.random.randint(key_of[10], (AREAS, SLOTS), 0, 2), jax.random.fold_in(key_of[10], 1), 0, 1).astype(jnp.int32)
    return dict(initial_rates=initial_rates, prior_rates=prior_rates, local_weight=local_weight, long_weight=long_weight, input_weight=input_weight, unit_bias=unit_bias, leak_rate=leak_rate, stimulus=stimulus, link_source=link_source, link_block=link_block, link_delay=link_delay)


def per_area(weights, factors):
    return lax.map(lambda operands: jnp.dot(operands[0], operands[1], preferred_element_type=jnp.float32), (weights, factors))


def pick_inputs(earlier, later_copy, link_source, link_block, link_delay):
    block_count = UNITS // BLOCK
    history = jnp.stack([later_copy, earlier], axis=1).reshape(AREAS, 2 * block_count, BLOCK, TRIALS)
    flat_rows = (link_delay * block_count + link_block).astype(jnp.int32)
    picked = history[link_source.astype(jnp.int32), flat_rows]
    return picked.reshape(AREAS, SLOTS * BLOCK, TRIALS)


def update(state_now, copy_now, current, stim_now, local_weight, input_weight, unit_bias, leak_rate):
    drive_sum = per_area(local_weight, copy_now) + current
    drive_sum = drive_sum + jnp.einsum("aus,st->aut", input_weight.astype(jnp.float32), stim_now.astype(jnp.float32))
    drive_sum = drive_sum + unit_bias[:, :, None]
    return state_now + leak_rate[:, :, None] * (jnp.tanh(drive_sum) - state_now)


def reference(initial_rates, prior_rates, local_weight, long_weight, input_weight, unit_bias, leak_rate, stimulus, link_source, link_block, link_delay):
    state_now = initial_rates
    later_copy = initial_rates.astype(jnp.bfloat16)
    earlier = prior_rates
    for window in range(WINDOWS):
        current = per_area(long_weight, pick_inputs(earlier, later_copy, link_source, link_block, link_delay))
        state_now = update(state_now, later_copy, current, stimulus[2 * window], local_weight, input_weight, unit_bias, leak_rate)
        earlier = state_now.astype(jnp.bfloat16)
        state_now = update(state_now, earlier, current, stimulus[2 * window + 1], local_weight, input_weight, unit_bias, leak_rate)
        later_copy = state_now.astype(jnp.bfloat16)
    final_current = per_area(long_weight, pick_inputs(earlier, later_copy, link_source, link_block, link_delay))
    return state_now, final_current
```

```python
import jax
import jax.numpy as jnp
from jax import lax
from jax.sharding import PartitionSpec as P

UNITS = 4096
BLOCK = 128
WINDOWS = 3


def shards(
    initial_rates,
    prior_rates,
    local_weight,
    long_weight,
    input_weight,
    unit_bias,
    leak_rate,
    stimulus,
    link_source,
    link_block,
    link_delay,
):
    areas_all, slot_count = link_source.shape
    per_pair = max(1, -(-slot_count // areas_all))
    blocks_per_area = UNITS // BLOCK
    area_here = lax.axis_index("area")
    slot_order = jnp.arange(slot_count, dtype=jnp.int32)
    same_source = (link_source[:, :, None] == link_source[:, None, :]) & (
        slot_order[None, None, :] < slot_order[None, :, None]
    )
    pair_index = jnp.sum(same_source.astype(jnp.int32), axis=2)
    block_row = link_delay * blocks_per_area + link_block
    from_here = link_source == area_here
    pair_range = jnp.arange(per_pair, dtype=jnp.int32)
    matched = from_here[:, None, :] & (pair_index[:, None, :] == pair_range[None, :, None])
    send_rows = jnp.sum(jnp.where(matched, block_row[:, None, :], 0), axis=2).reshape(-1)
    send_block = send_rows % blocks_per_area
    send_delay = send_rows // blocks_per_area
    own_source = lax.dynamic_index_in_dim(link_source, area_here, 0, keepdims=False)
    own_pair = lax.dynamic_index_in_dim(pair_index, area_here, 0, keepdims=False)
    take_rows = own_source * per_pair + own_pair
    weight_local = local_weight[0]
    weight_long = long_weight[0]
    weight_input = input_weight[0]
    bias_row = unit_bias[0]
    leak_row = leak_rate[0]

    def long_range(earlier_full, later_full):
        piece_rows = BLOCK // lax.axis_size("unit")
        trials = later_full.shape[-1]
        first_row = lax.axis_index("unit") * piece_rows

        def piece(slot):
            start = (send_block[slot] * BLOCK + first_row, 0)
            size = (piece_rows, trials)
            later_piece = lax.dynamic_slice(later_full, start, size)
            earlier_piece = lax.dynamic_slice(earlier_full, start, size)
            return jnp.where(send_delay[slot] == 0, later_piece, earlier_piece)

        outgoing = jnp.stack([piece(slot) for slot in range(areas_all * per_pair)])
        arrived = lax.all_to_all(outgoing, "area", split_axis=0, concat_axis=0, tiled=True)
        inputs = jnp.concatenate(
            [lax.dynamic_slice_in_dim(arrived, take_rows[slot], 1, 0) for slot in range(slot_count)]
        )
        inputs = lax.all_gather(inputs, "unit", axis=1, tiled=True)
        inputs = inputs.reshape(-1, inputs.shape[-1])
        return jnp.dot(weight_long, inputs, preferred_element_type=jnp.float32)

    def share_rates(state_now):
        return lax.all_gather(state_now.astype(jnp.bfloat16), "unit", axis=0, tiled=True)

    def update(state_now, shared, current, index_now):
        drive_sum = jnp.dot(weight_local, shared, preferred_element_type=jnp.float32) + current
        drive_sum = drive_sum + jnp.dot(
            weight_input, stimulus[index_now], preferred_element_type=jnp.float32
        )
        drive_sum = drive_sum + bias_row[:, None]
        return state_now + leak_row[:, None] * (jnp.tanh(drive_sum) - state_now)

    state_now = initial_rates[0]
    earlier_full = lax.all_gather(prior_rates[0], "unit", axis=0, tiled=True)
    later_full = share_rates(state_now)
    for window in range(WINDOWS):
        current = long_range(earlier_full, later_full)
        state_now = update(state_now, later_full, current, 2 * window)
        earlier_full = share_rates(state_now)
        state_now = update(state_now, earlier_full, current, 2 * window + 1)
        later_full = share_rates(state_now)
    final_current = long_range(earlier_full, later_full)
    return (state_now[None], final_current[None])


def solution(mesh):
    return jax.shard_map(
        shards,
        mesh=mesh,
        in_specs=(
            P("area", "unit", None),
            P("area", "unit", None),
            P("area", "unit", None),
            P("area", "unit", None),
            P("area", "unit", None),
            P("area", "unit"),
            P("area", "unit"),
            P(),
            P(),
            P(),
            P(),
        ),
        out_specs=(P("area", "unit", None), P("area", "unit", None)),
        check_vma=False,
    )
```

```python
import functools

import jax
import jax.numpy as jnp
from jax import lax
from jax.experimental import pallas as pl
from jax.experimental.pallas import tpu as pltpu
from jax.sharding import PartitionSpec as P

BLOCK = 128
HALF = BLOCK // 2
WINDOWS = 3
CORES = 2
CHUNKS = 2
EXCHANGES = WINDOWS + 1
GENERATIONS = 2 * EXCHANGES


def kernel(n_area, n_unit, per_pair, slots, *refs):
    (send_block, send_delay, take_rows, start_ref, prior_ref, local_hbm, long_hbm,
     input_ref, bias_ref, leak_ref, stim_ref, rates, current) = refs[:13]
    full = refs[13 : 13 + GENERATIONS]
    inbox = refs[13 + GENERATIONS : 13 + GENERATIONS + EXCHANGES]
    (local_w, long_w, outbox, inputs, drive, weight_sem, share_send, share_recv,
     block_send, block_recv, pass_send, pass_recv) = refs[13 + GENERATIONS + EXCHANGES :]
    rows, trials = rates.shape
    chips = n_unit // CORES
    shard = rows // HALF
    part = shard // CHUNKS
    tile = rows // CHUNKS
    area, unit = lax.axis_index("area"), lax.axis_index("unit")
    chip, core = unit // CORES, unit % CORES
    sibling = chip * CORES + (1 - core)

    def chip_at(offset):
        return lax.rem(chip + offset + chips, chips)

    def area_at(offset):
        return lax.rem(area + offset + n_area, n_area)

    loads = [
        pltpu.make_async_copy(
            local_hbm.at[:, pl.ds(u * rows, rows)], local_w.at[u], weight_sem.at[u]
        )
        for u in range(n_unit)
    ]
    loads.append(pltpu.make_async_copy(long_hbm, long_w, weight_sem.at[n_unit]))
    for load in loads:
        load.start()

    barrier = pltpu.get_barrier_semaphore()
    pl.semaphore_signal(barrier, inc=1, device_id={"unit": sibling})
    for j in range(1, chips):
        pl.semaphore_signal(barrier, inc=1, device_id={"unit": chip_at(j) * CORES + core})

    @pl.loop(1, n_area)
    def _(d):
        pl.semaphore_signal(barrier, inc=1, device_id={"area": area_at(d)})

    pl.semaphore_wait(barrier, 1 + (chips - 1) + (n_area - 1))

    def share(g, k, lane):
        if lane == 0:
            owner, target = unit, sibling
        elif lane < chips:
            owner, target = unit, chip_at(lane) * CORES + core
        else:
            owner, target = chip_at(-(lane - chips + 1)) * CORES + core, sibling
        place = full[g].at[pl.ds(owner * shard + k * part, part)]
        return pltpu.make_async_remote_copy(
            src_ref=place,
            dst_ref=place,
            send_sem=share_send.at[g % 2, k, lane],
            recv_sem=share_recv.at[g, k, lane],
            device_id={"unit": target},
        )

    lanes = 2 * chips - 1

    def share_out(g, k):
        for lane in range(1, chips):
            share(g, k, lane).start()
        share(g, k, 0).start()

    def hand_on(g):
        for k in range(CHUNKS):
            for j in range(1, chips):
                share(g, k, j).wait_recv()
                share(g, k, chips - 1 + j).start()

    def wait_lane(g, lane):
        for k in range(CHUNKS):
            share(g, k, lane).wait_recv()

    def sends_done(g):
        for k in range(CHUNKS):
            for lane in range(lanes):
                share(g, k, lane).wait_send()

    def copy_of(g, owner):
        return full[g][pl.ds(owner * shard, shard)].reshape(rows, trials)

    def product(g, owner, at):
        return jnp.dot(local_w[owner, at, :], copy_of(g, owner), preferred_element_type=jnp.float32)

    def span(k):
        return pl.ds(pl.multiple_of(k * tile, tile), tile)

    def begin(g, n):
        @pl.loop(0, CHUNKS)
        def _(k):
            at = span(k)
            given = jnp.dot(input_ref[at, :], stim_ref[n], preferred_element_type=jnp.float32)
            drive[at, :] = product(g, unit, at) + given + bias_ref[at, :]

    def add(g, owner):
        @pl.loop(0, CHUNKS)
        def _(k):
            at = span(k)
            drive[at, :] += product(g, owner, at)

    def long_product(at):
        return jnp.dot(
            long_w[at, :], inputs[...].reshape(slots * BLOCK, trials),
            preferred_element_type=jnp.float32,
        )

    def settle(g, k, total):
        at = pl.ds(k * tile, tile)
        old = rates[at, :]
        new = old + leak_ref[at, :] * (jnp.tanh(total) - old)
        rates[at, :] = new
        full[g + 1][pl.ds(unit * shard + k * part, part)] = new.astype(jnp.bfloat16).reshape(
            part, HALF, trials
        )
        share_out(g + 1, k)

    def pick(e, entry, half):
        where = send_block[entry] * 2 + half
        earlier, later = full[2 * e][where], full[2 * e + 1][where]
        return jnp.where(send_delay[entry] == 0, later, earlier)

    def outgoing(e, d):
        target = area_at(d)
        return pltpu.make_async_remote_copy(
            src_ref=outbox.at[pl.ds(target * per_pair, per_pair)],
            dst_ref=inbox[e].at[core, pl.ds(area * per_pair, per_pair)],
            send_sem=block_send.at[d],
            recv_sem=block_recv.at[e, d],
            device_id={"area": target},
        )

    def passing(e, d):
        place = inbox[e].at[core, pl.ds(area_at(-d) * per_pair, per_pair)]
        return pltpu.make_async_remote_copy(
            src_ref=place,
            dst_ref=place,
            send_sem=pass_send.at[d],
            recv_sem=pass_recv.at[e, d],
            device_id={"unit": sibling},
        )

    def send_blocks(e):
        @pl.loop(1, n_area)
        def _(d):
            for p in range(per_pair):
                entry = area_at(d) * per_pair + p
                outbox[entry] = pick(e, entry, core)
            outgoing(e, d).start()

        for p in range(per_pair):
            entry = area * per_pair + p
            for half in range(2):
                inbox[e][half, entry] = pick(e, entry, half)

    def take_blocks(e):
        @pl.loop(1, n_area)
        def _(d):
            outgoing(e, d).wait_recv()
            passing(e, d).start()

        @pl.loop(1, n_area)
        def _(d):
            passing(e, d).wait_recv()
            passing(e, d).wait_send()
            outgoing(e, d).wait_send()

        @pl.loop(0, slots)
        def _(slot):
            for half in range(2):
                inputs[slot * 2 + half] = inbox[e][half, take_rows[slot]]

    away = [(chip_at(-j), chips - 1 + j) for j in range(1, chips)]

    rates[...] = start_ref[...]
    own = pl.ds(unit * shard, shard)
    full[1][own] = start_ref[...].astype(jnp.bfloat16).reshape(shard, HALF, trials)
    full[0][own] = prior_ref[...].reshape(shard, HALF, trials)
    for g in (1, 0):
        for k in range(CHUNKS):
            share_out(g, k)
    for load in loads:
        load.wait()

    for step in range(2 * WINDOWS):
        g = step + 1
        begin(g, step)
        wait_lane(g, 0)
        add(g, sibling)
        hand_on(g)
        if step == 0:
            hand_on(0)
            for lane in [0] + [lane for _, lane in away]:
                wait_lane(0, lane)
            sends_done(0)
        if step % 2 == 0:
            for _, lane in away:
                wait_lane(g, lane)
            send_blocks(step // 2)
            for source, _ in away:
                add(g, source * CORES + core)
                add(g, source * CORES + (1 - core))
            take_blocks(step // 2)
            for k in range(CHUNKS):
                at = pl.ds(k * tile, tile)
                now = long_product(at)
                current[at, :] = now
                settle(g, k, drive[at, :] + now)
        else:
            for source, _ in away:
                add(g, source * CORES + core)
            for source, lane in away[:-1]:
                wait_lane(g, lane)
                add(g, source * CORES + (1 - core))
            source, lane = away[-1]
            wait_lane(g, lane)
            for k in range(CHUNKS):
                at = pl.ds(k * tile, tile)
                total = drive[at, :] + product(g, source * CORES + (1 - core), at)
                settle(g, k, total + current[at, :])
        sends_done(g)

    g = GENERATIONS - 1
    wait_lane(g, 0)
    hand_on(g)
    for _, lane in away:
        wait_lane(g, lane)
    send_blocks(WINDOWS)
    take_blocks(WINDOWS)
    for k in range(CHUNKS):
        at = pl.ds(k * tile, tile)
        current[at, :] = long_product(at)
    sends_done(g)


def shards(
    initial_rates,
    prior_rates,
    local_weight,
    long_weight,
    input_weight,
    unit_bias,
    leak_rate,
    stimulus,
    link_source,
    link_block,
    link_delay,
):
    areas_all, slot_count = link_source.shape
    per_pair = max(1, -(-slot_count // areas_all))
    n_area, n_unit = lax.axis_size("area"), lax.axis_size("unit")
    area_here = lax.axis_index("area")
    slot_order = jnp.arange(slot_count, dtype=jnp.int32)
    same_source = (link_source[:, :, None] == link_source[:, None, :]) & (
        slot_order[None, None, :] < slot_order[None, :, None]
    )
    pair_index = jnp.sum(same_source.astype(jnp.int32), axis=2)
    from_here = link_source == area_here
    pair_range = jnp.arange(per_pair, dtype=jnp.int32)
    matched = from_here[:, None, :] & (pair_index[:, None, :] == pair_range[None, :, None])
    send_block = jnp.sum(jnp.where(matched, link_block[:, None, :], 0), axis=2).reshape(-1)
    send_delay = jnp.sum(jnp.where(matched, link_delay[:, None, :], 0), axis=2).reshape(-1)
    own_source = lax.dynamic_index_in_dim(link_source, area_here, 0, keepdims=False)
    own_pair = lax.dynamic_index_in_dim(pair_index, area_here, 0, keepdims=False)
    take_rows = own_source * per_pair + own_pair

    rows, trials = initial_rates.shape[1:]
    units = local_weight.shape[2]
    pairs = areas_all * per_pair
    lanes = 2 * (n_unit // CORES) - 1
    smem = pl.BlockSpec(memory_space=pltpu.SMEM)
    vmem = pl.BlockSpec(memory_space=pltpu.VMEM)
    far = pl.BlockSpec(memory_space=pl.ANY)
    half_blocks = units // HALF
    dma = pltpu.SemaphoreType.DMA
    out = jax.ShapeDtypeStruct((rows, trials), jnp.float32)
    rates, current = pl.pallas_call(
        functools.partial(kernel, n_area, n_unit, per_pair, slot_count),
        out_shape=(out, out),
        in_specs=[smem] * 3 + [vmem] * 2 + [far] * 2 + [vmem] * 4,
        out_specs=(vmem, vmem),
        scratch_shapes=[pltpu.VMEM((half_blocks, HALF, trials), jnp.bfloat16)] * GENERATIONS
        + [pltpu.VMEM((2, pairs, HALF, trials), jnp.bfloat16)] * EXCHANGES
        + [
            pltpu.VMEM((n_unit, rows, rows), jnp.bfloat16),
            pltpu.VMEM((rows, slot_count * BLOCK), jnp.bfloat16),
            pltpu.VMEM((pairs, HALF, trials), jnp.bfloat16),
            pltpu.VMEM((2 * slot_count, HALF, trials), jnp.bfloat16),
            pltpu.VMEM((rows, trials), jnp.float32),
            dma((n_unit + 1,)),
            dma((2, CHUNKS, lanes)),
            dma((GENERATIONS, CHUNKS, lanes)),
            dma((n_area,)),
            dma((EXCHANGES, n_area)),
            dma((n_area,)),
            dma((EXCHANGES, n_area)),
        ],
        compiler_params=pltpu.CompilerParams(
            collective_id=0, has_side_effects=True, vmem_limit_bytes=48 * 2**20
        ),
    )(
        send_block, send_delay, take_rows, initial_rates[0], prior_rates[0],
        local_weight[0], long_weight[0], input_weight[0], unit_bias[0][:, None],
        leak_rate[0][:, None], stimulus,
    )
    return (rates[None], current[None])


def solution(mesh):
    return jax.shard_map(
        shards,
        mesh=mesh,
        in_specs=(
            P("area", "unit", None),
            P("area", "unit", None),
            P("area", "unit", None),
            P("area", "unit", None),
            P("area", "unit", None),
            P("area", "unit"),
            P("area", "unit"),
            P(),
            P(),
            P(),
            P(),
        ),
        out_specs=(P("area", "unit", None), P("area", "unit", None)),
        check_vma=False,
    )
```

```python
import functools

import jax
import jax.numpy as jnp
from jax import lax
from jax.experimental import pallas as pl
from jax.experimental.pallas import tpu as pltpu
from jax.sharding import PartitionSpec as P

BLOCK = 128
HALF = BLOCK // 2
WINDOWS = 3
CORES = 2
CHUNKS = 4
TILES = 2
EXCHANGES = WINDOWS + 1
GENERATIONS = 2 * EXCHANGES


def kernel(n_area, n_unit, per_pair, slots, *refs):
    (send_block, send_delay, take_rows, start_ref, prior_ref, local_hbm, long_hbm,
     input_ref, bias_ref, leak_ref, stim_ref, rates, current) = refs[:13]
    full = refs[13 : 13 + GENERATIONS]
    inbox = refs[13 + GENERATIONS : 13 + GENERATIONS + EXCHANGES]
    (local_w, long_w, outbox, inputs, drive, weight_sem, share_send, share_recv,
     block_send, block_recv, pass_send, pass_recv) = refs[13 + GENERATIONS + EXCHANGES :]
    rows, trials = rates.shape
    chips = n_unit // CORES
    shard = rows // HALF
    part = shard // CHUNKS
    tile = rows // TILES
    band = rows // CHUNKS
    area, unit = lax.axis_index("area"), lax.axis_index("unit")
    chip, core = unit // CORES, unit % CORES
    sibling = chip * CORES + (1 - core)

    def chip_at(offset):
        return lax.rem(chip + offset + chips, chips)

    def area_at(offset):
        return lax.rem(area + offset + n_area, n_area)

    loads = [
        pltpu.make_async_copy(
            local_hbm.at[:, pl.ds(u * rows, rows)], local_w.at[u], weight_sem.at[u]
        )
        for u in range(n_unit)
    ]
    loads.append(pltpu.make_async_copy(long_hbm, long_w, weight_sem.at[n_unit]))
    for load in loads:
        load.start()

    barrier = pltpu.get_barrier_semaphore()
    pl.semaphore_signal(barrier, inc=1, device_id={"unit": sibling})
    for j in range(1, chips):
        pl.semaphore_signal(barrier, inc=1, device_id={"unit": chip_at(j) * CORES + core})

    @pl.loop(1, n_area)
    def _(d):
        pl.semaphore_signal(barrier, inc=1, device_id={"area": area_at(d)})

    pl.semaphore_wait(barrier, 1 + (chips - 1) + (n_area - 1))

    def share(g, k, lane):
        if lane == 0:
            owner, target = unit, sibling
        elif lane < chips:
            owner, target = unit, chip_at(lane) * CORES + core
        else:
            owner, target = chip_at(-(lane - chips + 1)) * CORES + core, sibling
        place = full[g].at[pl.ds(owner * shard + k * part, part)]
        return pltpu.make_async_remote_copy(
            src_ref=place,
            dst_ref=place,
            send_sem=share_send.at[g % 2, k, lane],
            recv_sem=share_recv.at[g, k, lane],
            device_id={"unit": target},
        )

    lanes = 2 * chips - 1

    def share_out(g, k):
        for lane in range(1, chips):
            share(g, k, lane).start()
        share(g, k, 0).start()

    def hand_on(g):
        for k in range(CHUNKS):
            for j in range(1, chips):
                share(g, k, j).wait_recv()
                share(g, k, chips - 1 + j).start()

    def wait_lane(g, lane):
        for k in range(CHUNKS):
            share(g, k, lane).wait_recv()

    def sends_done(g):
        for k in range(CHUNKS):
            for lane in range(lanes):
                share(g, k, lane).wait_send()

    def copy_of(g, owner):
        return full[g][pl.ds(owner * shard, shard)].reshape(rows, trials)

    def product(g, owner, at):
        return jnp.dot(local_w[owner, at, :], copy_of(g, owner), preferred_element_type=jnp.float32)

    def span(k):
        return pl.ds(pl.multiple_of(k * tile, tile), tile)

    def begin(g, n):
        @pl.loop(0, TILES)
        def _(k):
            at = span(k)
            given = jnp.dot(input_ref[at, :], stim_ref[n], preferred_element_type=jnp.float32)
            drive[at, :] = product(g, unit, at) + given + bias_ref[at, :]

    def add(g, owner):
        @pl.loop(0, TILES)
        def _(k):
            at = span(k)
            drive[at, :] += product(g, owner, at)

    def long_product(at):
        return jnp.dot(
            long_w[at, :], inputs[...].reshape(slots * BLOCK, trials),
            preferred_element_type=jnp.float32,
        )

    def settle(g, k, total):
        at = pl.ds(k * band, band)
        old = rates[at, :]
        new = old + leak_ref[at, :] * (jnp.tanh(total) - old)
        rates[at, :] = new
        full[g + 1][pl.ds(unit * shard + k * part, part)] = new.astype(jnp.bfloat16).reshape(
            part, HALF, trials
        )
        share_out(g + 1, k)

    def pick(e, entry, half):
        where = send_block[entry] * 2 + half
        earlier, later = full[2 * e][where], full[2 * e + 1][where]
        return jnp.where(send_delay[entry] == 0, later, earlier)

    def outgoing(e, d):
        target = area_at(d)
        return pltpu.make_async_remote_copy(
            src_ref=outbox.at[pl.ds(target * per_pair, per_pair)],
            dst_ref=inbox[e].at[core, pl.ds(area * per_pair, per_pair)],
            send_sem=block_send.at[d],
            recv_sem=block_recv.at[e, d],
            device_id={"area": target},
        )

    def passing(e, d):
        place = inbox[e].at[core, pl.ds(area_at(-d) * per_pair, per_pair)]
        return pltpu.make_async_remote_copy(
            src_ref=place,
            dst_ref=place,
            send_sem=pass_send.at[d],
            recv_sem=pass_recv.at[e, d],
            device_id={"unit": sibling},
        )

    def send_blocks(e):
        @pl.loop(1, n_area)
        def _(d):
            for p in range(per_pair):
                entry = area_at(d) * per_pair + p
                outbox[entry] = pick(e, entry, core)
            outgoing(e, d).start()

        for p in range(per_pair):
            entry = area * per_pair + p
            for half in range(2):
                inbox[e][half, entry] = pick(e, entry, half)

    def take_blocks(e):
        @pl.loop(1, n_area)
        def _(d):
            outgoing(e, d).wait_recv()
            passing(e, d).start()

        @pl.loop(1, n_area)
        def _(d):
            passing(e, d).wait_recv()
            passing(e, d).wait_send()
            outgoing(e, d).wait_send()

        @pl.loop(0, slots)
        def _(slot):
            for half in range(2):
                inputs[slot * 2 + half] = inbox[e][half, take_rows[slot]]

    away = [(chip_at(-j), chips - 1 + j) for j in range(1, chips)]

    rates[...] = start_ref[...]
    own = pl.ds(unit * shard, shard)
    full[1][own] = start_ref[...].astype(jnp.bfloat16).reshape(shard, HALF, trials)
    full[0][own] = prior_ref[...].reshape(shard, HALF, trials)
    for g in (1, 0):
        for k in range(CHUNKS):
            share_out(g, k)
    for load in loads:
        load.wait()

    for step in range(2 * WINDOWS):
        g = step + 1
        begin(g, step)
        wait_lane(g, 0)
        add(g, sibling)
        hand_on(g)
        if step == 0:
            hand_on(0)
            for lane in [0] + [lane for _, lane in away]:
                wait_lane(0, lane)
            sends_done(0)
        if step % 2 == 0:
            for _, lane in away:
                wait_lane(g, lane)
            send_blocks(step // 2)
            for source, _ in away:
                add(g, source * CORES + core)
                add(g, source * CORES + (1 - core))
            take_blocks(step // 2)
            for k in range(CHUNKS):
                at = pl.ds(k * band, band)
                now = long_product(at)
                current[at, :] = now
                settle(g, k, drive[at, :] + now)
        else:
            for source, _ in away:
                add(g, source * CORES + core)
            for source, lane in away[:-1]:
                wait_lane(g, lane)
                add(g, source * CORES + (1 - core))
            source, lane = away[-1]
            wait_lane(g, lane)
            for k in range(CHUNKS):
                at = pl.ds(k * band, band)
                total = drive[at, :] + product(g, source * CORES + (1 - core), at)
                settle(g, k, total + current[at, :])
        sends_done(g)

    g = GENERATIONS - 1
    wait_lane(g, 0)
    hand_on(g)
    for _, lane in away:
        wait_lane(g, lane)
    send_blocks(WINDOWS)
    take_blocks(WINDOWS)
    for k in range(CHUNKS):
        at = pl.ds(k * band, band)
        current[at, :] = long_product(at)
    sends_done(g)


def shards(
    initial_rates,
    prior_rates,
    local_weight,
    long_weight,
    input_weight,
    unit_bias,
    leak_rate,
    stimulus,
    link_source,
    link_block,
    link_delay,
):
    areas_all, slot_count = link_source.shape
    per_pair = max(1, -(-slot_count // areas_all))
    n_area, n_unit = lax.axis_size("area"), lax.axis_size("unit")
    area_here = lax.axis_index("area")
    slot_order = jnp.arange(slot_count, dtype=jnp.int32)
    same_source = (link_source[:, :, None] == link_source[:, None, :]) & (
        slot_order[None, None, :] < slot_order[None, :, None]
    )
    pair_index = jnp.sum(same_source.astype(jnp.int32), axis=2)
    from_here = link_source == area_here
    pair_range = jnp.arange(per_pair, dtype=jnp.int32)
    matched = from_here[:, None, :] & (pair_index[:, None, :] == pair_range[None, :, None])
    send_block = jnp.sum(jnp.where(matched, link_block[:, None, :], 0), axis=2).reshape(-1)
    send_delay = jnp.sum(jnp.where(matched, link_delay[:, None, :], 0), axis=2).reshape(-1)
    own_source = lax.dynamic_index_in_dim(link_source, area_here, 0, keepdims=False)
    own_pair = lax.dynamic_index_in_dim(pair_index, area_here, 0, keepdims=False)
    take_rows = own_source * per_pair + own_pair

    rows, trials = initial_rates.shape[1:]
    units = local_weight.shape[2]
    pairs = areas_all * per_pair
    lanes = 2 * (n_unit // CORES) - 1
    smem = pl.BlockSpec(memory_space=pltpu.SMEM)
    vmem = pl.BlockSpec(memory_space=pltpu.VMEM)
    far = pl.BlockSpec(memory_space=pl.ANY)
    half_blocks = units // HALF
    dma = pltpu.SemaphoreType.DMA
    out = jax.ShapeDtypeStruct((rows, trials), jnp.float32)
    rates, current = pl.pallas_call(
        functools.partial(kernel, n_area, n_unit, per_pair, slot_count),
        out_shape=(out, out),
        in_specs=[smem] * 3 + [vmem] * 2 + [far] * 2 + [vmem] * 4,
        out_specs=(vmem, vmem),
        scratch_shapes=[pltpu.VMEM((half_blocks, HALF, trials), jnp.bfloat16)] * GENERATIONS
        + [pltpu.VMEM((2, pairs, HALF, trials), jnp.bfloat16)] * EXCHANGES
        + [
            pltpu.VMEM((n_unit, rows, rows), jnp.bfloat16),
            pltpu.VMEM((rows, slot_count * BLOCK), jnp.bfloat16),
            pltpu.VMEM((pairs, HALF, trials), jnp.bfloat16),
            pltpu.VMEM((2 * slot_count, HALF, trials), jnp.bfloat16),
            pltpu.VMEM((rows, trials), jnp.float32),
            dma((n_unit + 1,)),
            dma((2, CHUNKS, lanes)),
            dma((GENERATIONS, CHUNKS, lanes)),
            dma((n_area,)),
            dma((EXCHANGES, n_area)),
            dma((n_area,)),
            dma((EXCHANGES, n_area)),
        ],
        compiler_params=pltpu.CompilerParams(
            collective_id=0, has_side_effects=True, vmem_limit_bytes=48 * 2**20
        ),
    )(
        send_block, send_delay, take_rows, initial_rates[0], prior_rates[0],
        local_weight[0], long_weight[0], input_weight[0], unit_bias[0][:, None],
        leak_rate[0][:, None], stimulus,
    )
    return (rates[None], current[None])


def solution(mesh):
    return jax.shard_map(
        shards,
        mesh=mesh,
        in_specs=(
            P("area", "unit", None),
            P("area", "unit", None),
            P("area", "unit", None),
            P("area", "unit", None),
            P("area", "unit", None),
            P("area", "unit"),
            P("area", "unit"),
            P(),
            P(),
            P(),
            P(),
        ),
        out_specs=(P("area", "unit", None), P("area", "unit", None)),
        check_vma=False,
    )
```

```python
import functools

import jax
import jax.numpy as jnp
from jax import lax
from jax.experimental import pallas as pl
from jax.experimental.pallas import tpu as pltpu
from jax.sharding import PartitionSpec as P

BLOCK = 128
HALF = BLOCK // 2
WINDOWS = 3
CORES = 2
CHUNKS = 4
TILES = 2
EXCHANGES = WINDOWS + 1
GENERATIONS = 2 * EXCHANGES


def kernel(n_area, n_unit, per_pair, slots, *refs):
    (send_block, send_delay, take_rows, start_ref, prior_ref, local_hbm, long_hbm,
     input_ref, bias_ref, leak_ref, stim_ref, rates, current) = refs[:13]
    full = refs[13 : 13 + GENERATIONS]
    inbox = refs[13 + GENERATIONS : 13 + GENERATIONS + EXCHANGES]
    (local_w, long_w, outbox, inputs, drive, weight_sem, share_send, share_recv,
     block_send, block_recv, pass_send, pass_recv) = refs[13 + GENERATIONS + EXCHANGES :]
    rows, trials = rates.shape
    chips = n_unit // CORES
    shard = rows // HALF
    part = shard // CHUNKS
    tile = rows // TILES
    band = rows // CHUNKS
    area, unit = lax.axis_index("area"), lax.axis_index("unit")
    chip, core = unit // CORES, unit % CORES
    sibling = chip * CORES + (1 - core)

    def chip_at(offset):
        return lax.rem(chip + offset + chips, chips)

    def area_at(offset):
        return lax.rem(area + offset + n_area, n_area)

    own = pl.ds(unit * shard, shard)
    states = [
        pltpu.make_async_copy(start_ref, rates, weight_sem.at[n_unit + 1]),
        pltpu.make_async_copy(prior_ref, full[0].at[own], weight_sem.at[n_unit + 2]),
    ]
    loads = [
        pltpu.make_async_copy(
            local_hbm.at[:, pl.ds(u * rows, rows)], local_w.at[u], weight_sem.at[u]
        )
        for u in range(n_unit)
    ]
    loads.append(pltpu.make_async_copy(long_hbm, long_w, weight_sem.at[n_unit]))
    for load in states + loads:
        load.start()

    barrier = pltpu.get_barrier_semaphore()
    pl.semaphore_signal(barrier, inc=1, device_id={"unit": sibling})
    for j in range(1, chips):
        pl.semaphore_signal(barrier, inc=1, device_id={"unit": chip_at(j) * CORES + core})

    @pl.loop(1, n_area)
    def _(d):
        pl.semaphore_signal(barrier, inc=1, device_id={"area": area_at(d)})

    pl.semaphore_wait(barrier, 1 + (chips - 1) + (n_area - 1))

    def share(g, k, lane):
        if lane == 0:
            owner, target = unit, sibling
        elif lane < chips:
            owner, target = unit, chip_at(lane) * CORES + core
        else:
            owner, target = chip_at(-(lane - chips + 1)) * CORES + core, sibling
        place = full[g].at[pl.ds(owner * shard + k * part, part)]
        return pltpu.make_async_remote_copy(
            src_ref=place,
            dst_ref=place,
            send_sem=share_send.at[g % 2, k, lane],
            recv_sem=share_recv.at[g, k, lane],
            device_id={"unit": target},
        )

    lanes = 2 * chips - 1

    def share_out(g, k):
        for lane in range(1, chips):
            share(g, k, lane).start()
        share(g, k, 0).start()

    def hand_on(g):
        for k in range(CHUNKS):
            for j in range(1, chips):
                share(g, k, j).wait_recv()
                share(g, k, chips - 1 + j).start()

    def wait_lane(g, lane):
        for k in range(CHUNKS):
            share(g, k, lane).wait_recv()

    def sends_done(g):
        for k in range(CHUNKS):
            for lane in range(lanes):
                share(g, k, lane).wait_send()

    def copy_of(g, owner):
        return full[g][pl.ds(owner * shard, shard)].reshape(rows, trials)

    def product(g, owner, at):
        return jnp.dot(local_w[owner, at, :], copy_of(g, owner), preferred_element_type=jnp.float32)

    def span(k):
        return pl.ds(pl.multiple_of(k * tile, tile), tile)

    def begin(g, n):
        @pl.loop(0, TILES)
        def _(k):
            at = span(k)
            given = jnp.dot(input_ref[at, :], stim_ref[n], preferred_element_type=jnp.float32)
            drive[at, :] = product(g, unit, at) + given + bias_ref[at, :]

    def add(g, owner):
        @pl.loop(0, TILES)
        def _(k):
            at = span(k)
            drive[at, :] += product(g, owner, at)

    def long_product(at):
        return jnp.dot(
            long_w[at, :], inputs[...].reshape(slots * BLOCK, trials),
            preferred_element_type=jnp.float32,
        )

    def settle(g, k, total):
        at = pl.ds(k * band, band)
        old = rates[at, :]
        new = old + leak_ref[at, :] * (jnp.tanh(total) - old)
        rates[at, :] = new
        full[g + 1][pl.ds(unit * shard + k * part, part)] = new.astype(jnp.bfloat16).reshape(
            part, HALF, trials
        )
        share_out(g + 1, k)

    def pick(e, entry, half):
        where = send_block[entry] * 2 + half
        earlier, later = full[2 * e][where], full[2 * e + 1][where]
        return jnp.where(send_delay[entry] == 0, later, earlier)

    def outgoing(e, d):
        target = area_at(d)
        return pltpu.make_async_remote_copy(
            src_ref=outbox.at[pl.ds(target * per_pair, per_pair)],
            dst_ref=inbox[e].at[core, pl.ds(area * per_pair, per_pair)],
            send_sem=block_send.at[d],
            recv_sem=block_recv.at[e, d],
            device_id={"area": target},
        )

    def passing(e, d):
        place = inbox[e].at[core, pl.ds(area_at(-d) * per_pair, per_pair)]
        return pltpu.make_async_remote_copy(
            src_ref=place,
            dst_ref=place,
            send_sem=pass_send.at[d],
            recv_sem=pass_recv.at[e, d],
            device_id={"unit": sibling},
        )

    def send_blocks(e):
        @pl.loop(1, n_area)
        def _(d):
            for p in range(per_pair):
                entry = area_at(d) * per_pair + p
                outbox[entry] = pick(e, entry, core)
            outgoing(e, d).start()

        for p in range(per_pair):
            entry = area * per_pair + p
            for half in range(2):
                inbox[e][half, entry] = pick(e, entry, half)

    def take_blocks(e):
        @pl.loop(1, n_area)
        def _(d):
            outgoing(e, d).wait_recv()
            passing(e, d).start()

        @pl.loop(1, n_area)
        def _(d):
            passing(e, d).wait_recv()
            passing(e, d).wait_send()
            outgoing(e, d).wait_send()

        @pl.loop(0, slots)
        def _(slot):
            for half in range(2):
                inputs[slot * 2 + half] = inbox[e][half, take_rows[slot]]

    away = [(chip_at(-j), chips - 1 + j) for j in range(1, chips)]

    for load in states:
        load.wait()
    full[1][own] = rates[...].astype(jnp.bfloat16).reshape(shard, HALF, trials)
    for g in (1, 0):
        for k in range(CHUNKS):
            share_out(g, k)
    for load in loads:
        load.wait()

    for step in range(2 * WINDOWS):
        g = step + 1
        begin(g, step)
        wait_lane(g, 0)
        add(g, sibling)
        hand_on(g)
        if step == 0:
            hand_on(0)
            for lane in [0] + [lane for _, lane in away]:
                wait_lane(0, lane)
            sends_done(0)
        if step % 2 == 0:
            for _, lane in away:
                wait_lane(g, lane)
            send_blocks(step // 2)
            for source, _ in away:
                add(g, source * CORES + core)
                add(g, source * CORES + (1 - core))
            take_blocks(step // 2)
            for k in range(CHUNKS):
                at = pl.ds(k * band, band)
                now = long_product(at)
                current[at, :] = now
                settle(g, k, drive[at, :] + now)
        else:
            for source, _ in away:
                add(g, source * CORES + core)
            for source, lane in away[:-1]:
                wait_lane(g, lane)
                add(g, source * CORES + (1 - core))
            source, lane = away[-1]
            wait_lane(g, lane)
            for k in range(CHUNKS):
                at = pl.ds(k * band, band)
                total = drive[at, :] + product(g, source * CORES + (1 - core), at)
                settle(g, k, total + current[at, :])
        sends_done(g)

    g = GENERATIONS - 1
    wait_lane(g, 0)
    hand_on(g)
    for _, lane in away:
        wait_lane(g, lane)
    send_blocks(WINDOWS)
    take_blocks(WINDOWS)
    for k in range(CHUNKS):
        at = pl.ds(k * band, band)
        current[at, :] = long_product(at)
    sends_done(g)


def shards(
    initial_rates,
    prior_rates,
    local_weight,
    long_weight,
    input_weight,
    unit_bias,
    leak_rate,
    stimulus,
    link_source,
    link_block,
    link_delay,
):
    areas_all, slot_count = link_source.shape
    per_pair = max(1, -(-slot_count // areas_all))
    n_area, n_unit = lax.axis_size("area"), lax.axis_size("unit")
    area_here = lax.axis_index("area")
    slot_order = jnp.arange(slot_count, dtype=jnp.int32)
    same_source = (link_source[:, :, None] == link_source[:, None, :]) & (
        slot_order[None, None, :] < slot_order[None, :, None]
    )
    pair_index = jnp.sum(same_source.astype(jnp.int32), axis=2)
    from_here = link_source == area_here
    pair_range = jnp.arange(per_pair, dtype=jnp.int32)
    matched = from_here[:, None, :] & (pair_index[:, None, :] == pair_range[None, :, None])
    send_block = jnp.sum(jnp.where(matched, link_block[:, None, :], 0), axis=2).reshape(-1)
    send_delay = jnp.sum(jnp.where(matched, link_delay[:, None, :], 0), axis=2).reshape(-1)
    own_source = lax.dynamic_index_in_dim(link_source, area_here, 0, keepdims=False)
    own_pair = lax.dynamic_index_in_dim(pair_index, area_here, 0, keepdims=False)
    take_rows = own_source * per_pair + own_pair

    rows, trials = initial_rates.shape[1:]
    units = local_weight.shape[2]
    pairs = areas_all * per_pair
    lanes = 2 * (n_unit // CORES) - 1
    smem = pl.BlockSpec(memory_space=pltpu.SMEM)
    vmem = pl.BlockSpec(memory_space=pltpu.VMEM)
    far = pl.BlockSpec(memory_space=pl.ANY)
    half_blocks = units // HALF
    dma = pltpu.SemaphoreType.DMA
    out = jax.ShapeDtypeStruct((rows, trials), jnp.float32)
    rates, current = pl.pallas_call(
        functools.partial(kernel, n_area, n_unit, per_pair, slot_count),
        out_shape=(out, out),
        in_specs=[smem] * 3 + [far] * 4 + [vmem] * 4,
        out_specs=(vmem, vmem),
        scratch_shapes=[pltpu.VMEM((half_blocks, HALF, trials), jnp.bfloat16)] * GENERATIONS
        + [pltpu.VMEM((2, pairs, HALF, trials), jnp.bfloat16)] * EXCHANGES
        + [
            pltpu.VMEM((n_unit, rows, rows), jnp.bfloat16),
            pltpu.VMEM((rows, slot_count * BLOCK), jnp.bfloat16),
            pltpu.VMEM((pairs, HALF, trials), jnp.bfloat16),
            pltpu.VMEM((2 * slot_count, HALF, trials), jnp.bfloat16),
            pltpu.VMEM((rows, trials), jnp.float32),
            dma((n_unit + 3,)),
            dma((2, CHUNKS, lanes)),
            dma((GENERATIONS, CHUNKS, lanes)),
            dma((n_area,)),
            dma((EXCHANGES, n_area)),
            dma((n_area,)),
            dma((EXCHANGES, n_area)),
        ],
        compiler_params=pltpu.CompilerParams(
            collective_id=0, has_side_effects=True, vmem_limit_bytes=56 * 2**20
        ),
    )(
        send_block, send_delay, take_rows, initial_rates[0],
        prior_rates[0].reshape(rows // HALF, HALF, trials),
        local_weight[0], long_weight[0], input_weight[0], unit_bias[0][:, None],
        leak_rate[0][:, None], stimulus,
    )
    return (rates[None], current[None])


def solution(mesh):
    return jax.shard_map(
        shards,
        mesh=mesh,
        in_specs=(
            P("area", "unit", None),
            P("area", "unit", None),
            P("area", "unit", None),
            P("area", "unit", None),
            P("area", "unit", None),
            P("area", "unit"),
            P("area", "unit"),
            P(),
            P(),
            P(),
            P(),
        ),
        out_specs=(P("area", "unit", None), P("area", "unit", None)),
        check_vma=False,
    )
```
